256 devices in a mesh: seq: 32 (over y, z), head: 8 (over x, core).
Axes of the slice: x: 4, y: 4, z: 8, core: 2. Of those that a mesh axis runs over, the one named last changes fastest.
Arguments:
- queries: bfloat16 [32768, 4096], P(('seq', 'head')), may hold values from -8 to 8
- key_heads: bfloat16 [32768, 1024], P('seq', 'head'), may hold values from -8 to 8
- value_heads: bfloat16 [32768, 1024], P('seq', 'head'), may hold values from -6 to 6
- output_grad: bfloat16 [32768, 4096], P(('seq', 'head')), may hold values from -6 to 6
- doc_starts: int32 [32], replicated, may hold values from 0 to 32000, as said below
Outputs:
- attended: bfloat16 [32768, 4096], P(('seq', 'head'))
- query_grad: bfloat16 [32768, 4096], P(('seq', 'head'))
- key_grad: bfloat16 [32768, 1024], P('seq', 'head')
- value_grad: bfloat16 [32768, 1024], P('seq', 'head')
The draws below stay inside these ranges and needn't reach their ends.
Inputs may be any that keep to these rules, and one draw needn't show every extreme that they name: doc_starts[0] is 0 and the starts increase; every document has between half of 1024 and 1536 tokens, a multiple of 128, and the documents fill all 32768 tokens; some document has exactly 1536 tokens.
All inputs are finite; a program needn't handle non-finite values.
Results may differ from the reference program's by a relative error of at most 0.012.
The reference program's roundings to bfloat16 on the way (of `weights` and `d_score`) count: a program that leaves them out, or rounds other values in their place, can miss the bound.
Values may be sent and summed in bfloat16 or wider, within the bound.
A program may use at most 64 MiB of HBM per device.

```python
import jax
import jax.numpy as jnp
import numpy as np
from jax import lax

HEAD = 128
QH = 32
KVH = 8
TILE = 128
SHARD = 1024
MOST_DOC = 1536
TOKENS = 32768
NDOCS = 32


def draw_queries(key, part):
    key = jax.random.fold_in(key, 3)
    result = jnp.clip(jax.random.normal(key, (TOKENS, QH * HEAD), jnp.float32), -6.0, 6.0)
    return result.astype(jnp.bfloat16)


def draw_key_heads(key, part):
    key = jax.random.fold_in(key, 7)
    result = jnp.clip(jax.random.normal(key, (TOKENS, KVH * HEAD), jnp.float32), -6.0, 6.0)
    return result.astype(jnp.bfloat16)


def draw_doc_starts(key, part):
    key = jax.random.fold_in(key, 5)
    key_first, key_cut, key_pair, key_swap = jax.random.split(key, 4)
    tile_count = SHARD // TILE
    half_tiles = tile_count // 2
    pair_count = NDOCS // 2 - 2
    middle = NDOCS // 2
    forced_list = [number == 0 or middle - 3 <= 2 * number <= middle for number in range(pair_count)]
    forced = jnp.asarray(np.array(forced_list, dtype=bool))
    offset = jax.random.randint(key_first, (), max(1, half_tiles // 2), half_tiles).astype(jnp.int32)
    cut = jax.random.randint(key_cut, (pair_count,), 0, half_tiles).astype(jnp.int32)
    picked = jax.random.randint(key_pair, (pair_count,), half_tiles, 3 * half_tiles + 1).astype(jnp.int32)
    long_part = jnp.where(forced, 3 * half_tiles - cut, picked)
    short_part = 4 * half_tiles - long_part
    swapped = jax.random.randint(key_swap, (pair_count,), 0, 2) == 1
    first_part = jnp.where(swapped, short_part, long_part)
    second_part = jnp.where(swapped, long_part, short_part)
    pairs = jnp.stack([first_part, second_part], 1).reshape(-1)
    tail_step = half_tiles // 2
    head_piece = (half_tiles + offset).reshape(1)
    bridge = (2 * half_tiles + tail_step - offset).reshape(1)
    ending = jnp.array([3 * half_tiles, 2 * half_tiles - tail_step], jnp.int32)
    lengths = jnp.concatenate([head_piece, pairs, bridge, ending]).astype(jnp.int32)
    starts = (jnp.cumsum(lengths) - lengths) * TILE
    return starts.astype(jnp.int32)


def block_levels(stream_key, shape, pieces, least, high):
    def one(position, parts):
        steps = jax.random.uniform(jax.random.fold_in(jax.random.fold_in(stream_key, 6), position), (parts,), jnp.float32, least / len(pieces), high / len(pieces))
        return jnp.repeat(jnp.exp(steps), shape[position] // parts).reshape((-1,) + (1,) * (len(shape) - position - 1))

    factor_of = one(*pieces[0])
    for cut in pieces[1:]:
        factor_of = factor_of * one(*cut)
    return factor_of


def centred(own_key, shape, deviation, limit, pieces=(), kind=jnp.bfloat16):
    drawn = deviation * jax.random.normal(own_key, shape, jnp.float32)
    if pieces:
        drawn = drawn * block_levels(own_key, shape, pieces, -0.22, 0.18)
    return jnp.clip(drawn, -limit, limit).astype(kind)


def setup_inputs(seed: int = 0) -> dict:
    splits = jax.random.split(jax.random.key(seed), 6)
    return {
        "queries": draw_queries(jax.random.fold_in(splits[5], 71), 0),
        "key_heads": draw_key_heads(jax.random.fold_in(splits[5], 71), 0),
        "value_heads": centred(splits[2], (TOKENS, KVH * HEAD), 1.0, 6.0, ((0, 32), (1, 8))),
        "output_grad": centred(splits[3], (TOKENS, QH * HEAD), 1.0, 6.0, ((0, 256),)),
        "doc_starts": draw_doc_starts(jax.random.fold_in(splits[5], 71), 0),
    }


def doc_of(positions, doc_starts):
    passed = (positions[:, None] >= doc_starts[None, :]).astype(jnp.int32)
    return jnp.sum(passed, axis=1) - 1


def reference(queries, key_heads, value_heads, output_grad, doc_starts):
    group_size = QH // KVH
    row_count = min(512, SHARD // 2)
    reach_rows = MOST_DOC
    span_rows = reach_rows + row_count
    block_count = TOKENS // row_count
    factor = HEAD ** -0.5
    token_doc = doc_of(jnp.arange(TOKENS, dtype=jnp.int32), doc_starts)
    pad_doc = jnp.concatenate([jnp.full((reach_rows,), -1, jnp.int32), token_doc])
    pad_pos = jnp.arange(TOKENS + reach_rows, dtype=jnp.int32) - reach_rows
    q_all = queries.reshape(TOKENS, KVH, group_size, HEAD)
    g_all = output_grad.reshape(TOKENS, KVH, group_size, HEAD)
    k_all = key_heads.reshape(TOKENS, KVH, HEAD)
    v_all = value_heads.reshape(TOKENS, KVH, HEAD)
    padding = jnp.zeros((reach_rows, HEAD), jnp.bfloat16)

    def one_group(number):
        q_group = lax.dynamic_index_in_dim(q_all, number, 1, keepdims=False)
        g_group = lax.dynamic_index_in_dim(g_all, number, 1, keepdims=False)
        k_padded = jnp.concatenate([padding, lax.dynamic_index_in_dim(k_all, number, 1, keepdims=False)], 0)
        v_padded = jnp.concatenate([padding, lax.dynamic_index_in_dim(v_all, number, 1, keepdims=False)], 0)

        def block_step(carried, block_number):
            k_sum, v_sum = carried
            row_start = block_number * row_count
            q_rows = lax.dynamic_slice_in_dim(q_group, row_start, row_count, 0).astype(jnp.float32)
            g_rows = lax.dynamic_slice_in_dim(g_group, row_start, row_count, 0).astype(jnp.float32)
            k_rows = lax.dynamic_slice_in_dim(k_padded, row_start, span_rows, 0).astype(jnp.float32)
            v_rows = lax.dynamic_slice_in_dim(v_padded, row_start, span_rows, 0).astype(jnp.float32)
            q_doc = lax.dynamic_slice_in_dim(token_doc, row_start, row_count, 0)
            q_pos = row_start + jnp.arange(row_count, dtype=jnp.int32)
            k_doc = lax.dynamic_slice_in_dim(pad_doc, row_start, span_rows, 0)
            k_pos = lax.dynamic_slice_in_dim(pad_pos, row_start, span_rows, 0)
            allowed = (q_doc[:, None] == k_doc[None, :]) & (k_pos[None, :] <= q_pos[:, None])
            scores = jnp.einsum("qjd,kd->jqk", q_rows, k_rows) * factor
            scores = jnp.where(allowed[None], scores, -jnp.inf)
            log_total = jax.nn.logsumexp(scores, axis=-1)
            exact = jnp.exp(scores - log_total[..., None])
            weights = lax.optimization_barrier(exact.astype(jnp.bfloat16)).astype(jnp.float32)
            attend_rows = lax.optimization_barrier(jnp.einsum("jqk,kd->qjd", weights, v_rows).astype(jnp.bfloat16))
            row_delta = jnp.sum(g_rows * attend_rows.astype(jnp.float32), axis=-1)
            d_prob = jnp.einsum("qjd,kd->jqk", g_rows, v_rows)
            d_score = exact * (d_prob - row_delta.T[..., None])
            d_score = lax.optimization_barrier(d_score.astype(jnp.bfloat16)).astype(jnp.float32)
            d_query = (jnp.einsum("jqk,kd->qjd", d_score, k_rows) * factor).astype(jnp.bfloat16)
            k_part = jnp.einsum("jqk,qjd->kd", d_score, q_rows)
            v_part = jnp.einsum("jqk,qjd->kd", weights, g_rows)
            k_sum = lax.dynamic_update_slice_in_dim(k_sum, lax.dynamic_slice_in_dim(k_sum, row_start, span_rows, 0) + k_part, row_start, 0)
            v_sum = lax.dynamic_update_slice_in_dim(v_sum, lax.dynamic_slice_in_dim(v_sum, row_start, span_rows, 0) + v_part, row_start, 0)
            return (k_sum, v_sum), (attend_rows, d_query)

        initial = (jnp.zeros((TOKENS + reach_rows, HEAD), jnp.float32), jnp.zeros((TOKENS + reach_rows, HEAD), jnp.float32))
        (k_sum, v_sum), (attend_rows, d_query) = lax.scan(block_step, initial, jnp.arange(block_count, dtype=jnp.int32))
        key_part = (k_sum[reach_rows:] * factor).astype(jnp.bfloat16)
        value_part = v_sum[reach_rows:].astype(jnp.bfloat16)
        return attend_rows, d_query, key_part, value_part

    attend_all, query_all, key_all, value_all = lax.map(one_group, jnp.arange(KVH, dtype=jnp.int32))
    attended = attend_all.reshape(KVH, TOKENS, group_size, HEAD).transpose(1, 0, 2, 3).reshape(TOKENS, QH * HEAD)
    query_grad = query_all.reshape(KVH, TOKENS, group_size, HEAD).transpose(1, 0, 2, 3).reshape(TOKENS, QH * HEAD)
    key_grad = key_all.transpose(1, 0, 2).reshape(TOKENS, KVH * HEAD)
    value_grad = value_all.transpose(1, 0, 2).reshape(TOKENS, KVH * HEAD)
    return attended, query_grad, key_grad, value_grad
```

```python
import functools
import math

import jax
import jax.numpy as jnp
from jax import lax
from jax.experimental import pallas as pl
from jax.experimental.pallas import tpu as pltpu
from jax.sharding import PartitionSpec as P

HEAD = 128
QH = 32
KVH = 8
TILE = 128
SHARD = 1024
REACH = 11
WIN = REACH + 1
GROUP = QH // KVH
COLS = GROUP * HEAD
TILES = SHARD // TILE
NEAR = SHARD
FAR = REACH * TILE - SHARD
BACK = NEAR + FAR
ROWS = BACK + SHARD
CHUNK = 256
FACTOR = HEAD**-0.5
SCALE = FACTOR * math.log2(math.e)
LOW = -1e30
F32 = jnp.float32
BF16 = jnp.bfloat16
MESH = pl.DeviceIdType.MESH


def mm(a, b):
    return jnp.dot(a, b, preferred_element_type=F32)


def fold(x, op):
    return op(x.reshape(x.shape[0] // 8, 8, x.shape[1]), axis=0)


def flip(x):
    return jnp.concatenate([x[:, h * HEAD : (h + 1) * HEAD].T for h in range(GROUP)], axis=1)


def stack(x):
    return jnp.concatenate([x[:, h * HEAD : (h + 1) * HEAD] for h in range(GROUP)], axis=0)


def attend(base, bias, q, g, k_win, v_win, k_flip, v_flip, k_sum, v_sum, s_buf, p_buf, d_buf):
    q_flip, q_rows = flip(q), stack(q)
    count = WIN * TILE // CHUNK
    per = CHUNK // TILE
    top = jnp.full((8, COLS), LOW, F32)
    for c in range(count):
        s = mm(k_win[pl.ds(base + c * CHUNK, CHUNK), :], q_flip)
        if c == count - 1:
            key = lax.broadcasted_iota(jnp.int32, (TILE, COLS), 0)
            tok = lax.broadcasted_iota(jnp.int32, (TILE, COLS), 1) % TILE
            last = jnp.where(key <= tok, s[CHUNK - TILE :], LOW)
            s = jnp.concatenate([s[: CHUNK - TILE], last], axis=0)
        s_buf[c * CHUNK : (c + 1) * CHUNK, :] = s
        for u in range(per):
            top = jnp.maximum(top, fold(s[u * TILE : (u + 1) * TILE], jnp.max) + bias[c * per + u])
    top = jnp.max(top, axis=0, keepdims=True)
    total = jnp.zeros((8, COLS), F32)
    for c in range(WIN):
        rows = slice(c * TILE, (c + 1) * TILE)
        p = jnp.exp2((s_buf[rows, :] - (top - bias[c])) * SCALE)
        total = total + fold(p, jnp.sum)
        p_buf[rows, :] = p.astype(BF16)
    inverse = 1.0 / jnp.sum(total, axis=0, keepdims=True)
    out = (mm(v_flip[:, pl.ds(base, WIN * TILE)], p_buf[...]) * inverse).astype(BF16)
    g_flip = (flip(g).astype(F32) * inverse).astype(BF16)
    g_rows = stack(flip(g_flip))
    delta = jnp.sum(g_flip.astype(F32) * out.astype(F32), axis=0, keepdims=True)
    for c in range(count):
        rows = slice(c * CHUNK, (c + 1) * CHUNK)
        keys = pl.ds(base + c * CHUNK, CHUNK)
        p = p_buf[rows, :]
        d_prob = mm(v_win[keys, :], g_flip)
        d_score = (p.astype(F32) * (d_prob - delta)).astype(BF16)
        d_buf[rows, :] = d_score
        v_sum[keys, :] += mm(p, g_rows)
        k_sum[keys, :] += mm(d_score, q_rows)
    d_query = (mm(k_flip[:, pl.ds(base, WIN * TILE)], d_buf[...]) * FACTOR).astype(BF16)
    return flip(out), flip(d_query)


def kernel(
    seqs, starts, q_in, k_in, v_in, g_in, o_out, dq_out, dk_out, dv_out,
    q_buf, g_buf, o_buf, dq_buf, k_win, v_win, k_flip, v_flip, k_sum, v_sum, s_buf, p_buf, d_buf,
    k_part, v_part, k_near, v_near, k_far, v_far,
    in_send, q_recv, g_recv, out_send, o_recv, dq_recv, z_send, z_recv,
):
    s, h = lax.axis_index("seq"), lax.axis_index("head")
    x, core = h // 2, h % 2

    def head_of(dx, dc):
        return ((x + dx) % 4) * 2 + (core + dc) % 2

    def seq_of(by):
        return (s + by + seqs) % seqs

    barrier = pltpu.get_barrier_semaphore()
    others = [(s, head_of(dx, dc)) for dx in range(4) for dc in range(2) if dx or dc]
    others += [(seq_of(by), h) for by in (1, 2, -1, -2)]
    for other in others:
        pl.semaphore_signal(barrier, inc=1, device_id=other, device_id_type=MESH)
    pl.semaphore_wait(barrier, len(others))

    def cols(head):
        return pl.ds(pl.multiple_of(head * COLS, COLS), COLS)

    def send(src, dst, send_sem, recv_sem, to):
        copy = pltpu.make_async_remote_copy(
            src_ref=src, dst_ref=dst, send_sem=send_sem, recv_sem=recv_sem, device_id=to, device_id_type=MESH
        )
        copy.start()
        return copy

    kv = []
    for n, (src, dst) in enumerate(((k_in, k_win), (v_in, v_win))):
        kv.append(send(src, dst.at[pl.ds(FAR, NEAR)], z_send.at[n], z_recv.at[n], (seq_of(1), h)))
    for n, (src, dst) in enumerate(((k_in, k_win), (v_in, v_win))):
        kv.append(
            send(src.at[pl.ds(SHARD - FAR, FAR)], dst.at[pl.ds(0, FAR)], z_send.at[2 + n], z_recv.at[2 + n], (seq_of(2), h))
        )
    own = [
        pltpu.make_async_copy(k_in, k_win.at[pl.ds(BACK, SHARD)], z_recv.at[4]),
        pltpu.make_async_copy(v_in, v_win.at[pl.ds(BACK, SHARD)], z_recv.at[5]),
        pltpu.make_async_copy(q_in.at[:, cols(h)], q_buf.at[h], q_recv.at[h]),
        pltpu.make_async_copy(g_in.at[:, cols(h)], g_buf.at[h], g_recv.at[h]),
    ]
    for copy in own:
        copy.start()
    ins = []
    for n in range(1, 8):
        to = head_of(-(n // 2) + 4, n % 2)
        ins.append(send(q_in.at[:, cols(to)], q_buf.at[h], in_send.at[2 * n], q_recv.at[h], (s, to)))
        ins.append(send(g_in.at[:, cols(to)], g_buf.at[h], in_send.at[2 * n + 1], g_recv.at[h], (s, to)))

    k_sum[...] = jnp.zeros_like(k_sum)
    v_sum[...] = jnp.zeros_like(v_sum)
    own[0].wait()
    own[1].wait()
    for copy in kv:
        copy.wait_recv()

    def turn(j, carry):
        at = pl.ds(pl.multiple_of(j * TILE, TILE), TILE)
        k_flip[:, at] = k_win[at, :].T
        v_flip[:, at] = v_win[at, :].T
        return carry

    lax.fori_loop(0, ROWS // TILE, turn, 0)

    def arrived(buf, i, sem):
        pltpu.make_async_copy(buf.at[i], buf.at[i], sem.at[i]).wait()

    def step(r, carry):
        i = head_of(r // 2, r % 2)
        tile = s * TILES + i
        begin = jnp.int32(0)
        for n in range(starts.shape[0]):
            begin = jnp.maximum(begin, jnp.where(starts[n] <= tile * TILE, starts[n], 0))
        bias = [jnp.where((tile - REACH + c) * TILE >= begin, 0.0, LOW).astype(F32) for c in range(WIN)]
        arrived(q_buf, i, q_recv)
        arrived(g_buf, i, g_recv)
        out, d_query = attend(
            pl.multiple_of(i * TILE, TILE), bias, q_buf[i], g_buf[i], k_win, v_win, k_flip, v_flip, k_sum, v_sum,
            s_buf, p_buf, d_buf,
        )
        o_buf[i] = out
        dq_buf[i] = d_query

        @pl.when(r == 0)
        def _():
            pltpu.make_async_copy(o_buf.at[i], o_out.at[:, cols(h)], o_recv.at[h]).start()
            pltpu.make_async_copy(dq_buf.at[i], dq_out.at[:, cols(h)], dq_recv.at[h]).start()

        @pl.when(r > 0)
        def _():
            send(o_buf.at[i], o_out.at[:, cols(h)], out_send.at[2 * r], o_recv.at[h], (s, i))
            send(dq_buf.at[i], dq_out.at[:, cols(h)], out_send.at[2 * r + 1], dq_recv.at[h], (s, i))

        return carry

    lax.fori_loop(0, 8, step, 0)

    def part(j, carry):
        at = pl.ds(pl.multiple_of(j * TILE, TILE), TILE)
        k_part[at, :] = k_sum[at, :].astype(BF16)
        v_part[at, :] = v_sum[at, :].astype(BF16)
        return carry

    lax.fori_loop(0, BACK // TILE, part, 0)
    parts = []
    for n, (src, near, far) in enumerate(((k_part, k_near, k_far), (v_part, v_near, v_far))):
        parts.append(send(src.at[pl.ds(0, FAR)], far, z_send.at[4 + n], z_recv.at[6 + n], (seq_of(-2), h)))
        parts.append(send(src.at[pl.ds(FAR, NEAR)], near, z_send.at[6 + n], z_recv.at[8 + n], (seq_of(-1), h)))
    for copy in parts:
        copy.wait_recv()

    def total(j, carry):
        at = pl.ds(pl.multiple_of(j * TILE, TILE), TILE)
        full = pl.ds(pl.multiple_of(BACK + j * TILE, TILE), TILE)
        k_sum[full, :] += k_near[at, :].astype(F32)
        v_sum[full, :] += v_near[at, :].astype(F32)
        return carry

    lax.fori_loop(0, TILES, total, 0)

    def total_far(j, carry):
        at = pl.ds(pl.multiple_of(j * TILE, TILE), TILE)
        full = pl.ds(pl.multiple_of(ROWS - FAR + j * TILE, TILE), TILE)
        k_sum[full, :] += k_far[at, :].astype(F32)
        v_sum[full, :] += v_far[at, :].astype(F32)
        return carry

    lax.fori_loop(0, FAR // TILE, total_far, 0)
    dk_out[...] = (k_sum[pl.ds(BACK, SHARD), :] * FACTOR).astype(BF16)
    dv_out[...] = v_sum[pl.ds(BACK, SHARD), :].astype(BF16)

    for copy in kv + ins + parts:
        copy.wait_send()

    def finish(i, carry):
        pltpu.make_async_copy(o_buf.at[i], o_buf.at[i], o_recv.at[i]).wait()
        pltpu.make_async_copy(dq_buf.at[i], dq_buf.at[i], dq_recv.at[i]).wait()
        return carry

    lax.fori_loop(0, 8, finish, 0)

    def sent(n, carry):
        pltpu.make_async_copy(o_buf.at[0], o_buf.at[0], out_send.at[n]).wait()
        return carry

    lax.fori_loop(2, 16, sent, 0)


def local(seqs, queries, key_heads, value_heads, output_grad, doc_starts):
    vmem = pl.BlockSpec(memory_space=pltpu.VMEM)
    hbm = pl.BlockSpec(memory_space=pl.ANY)
    dma = pltpu.SemaphoreType.DMA
    return pl.pallas_call(
        functools.partial(kernel, seqs),
        out_shape=[
            jax.ShapeDtypeStruct(queries.shape, BF16),
            jax.ShapeDtypeStruct(queries.shape, BF16),
            jax.ShapeDtypeStruct(key_heads.shape, BF16),
            jax.ShapeDtypeStruct(key_heads.shape, BF16),
        ],
        in_specs=[pl.BlockSpec(memory_space=pltpu.SMEM), hbm, hbm, hbm, hbm],
        out_specs=[hbm, hbm, vmem, vmem],
        scratch_shapes=[pltpu.VMEM((TILES, TILE, COLS), BF16)] * 4
        + [pltpu.VMEM((ROWS, HEAD), BF16)] * 2
        + [pltpu.VMEM((HEAD, ROWS), BF16)] * 2
        + [pltpu.VMEM((ROWS, HEAD), F32)] * 2
        + [pltpu.VMEM((WIN * TILE, COLS), F32)]
        + [pltpu.VMEM((WIN * TILE, COLS), BF16)] * 2
        + [pltpu.VMEM((BACK, HEAD), BF16)] * 2
        + [pltpu.VMEM((NEAR, HEAD), BF16)] * 2
        + [pltpu.VMEM((FAR, HEAD), BF16)] * 2
        + [dma((16,)), dma((8,)), dma((8,)), dma((16,)), dma((8,)), dma((8,)), dma((8,)), dma((10,))],
        compiler_params=pltpu.CompilerParams(
            collective_id=0, has_side_effects=True, vmem_limit_bytes=48 << 20
        ),
        cost_estimate=pl.CostEstimate(flops=10**10, bytes_accessed=8 << 20, transcendentals=6 << 20),
        name="attention",
    )(doc_starts, queries, key_heads, value_heads, output_grad)


def solution(mesh):
    wide = P(("seq", "head"), None)
    narrow = P("seq", "head")
    return jax.shard_map(
        functools.partial(local, mesh.shape["seq"]),
        mesh=mesh,
        in_specs=(wide, narrow, narrow, wide, P()),
        out_specs=(wide, wide, narrow, narrow),
        check_vma=False,
    )
```

```python
import functools
import math

import jax
import jax.numpy as jnp
from jax import lax
from jax.experimental import pallas as pl
from jax.experimental.pallas import tpu as pltpu
from jax.sharding import PartitionSpec as P

HEAD = 128
QH = 32
KVH = 8
TILE = 128
SHARD = 1024
REACH = 11
WIN = REACH + 1
GROUP = QH // KVH
COLS = GROUP * HEAD
TILES = SHARD // TILE
NEAR = SHARD
FAR = REACH * TILE - SHARD
BACK = NEAR + FAR
ROWS = BACK + SHARD
CHUNK = 256
FACTOR = HEAD**-0.5
SCALE = FACTOR * math.log2(math.e)
LOW = -1e30
F32 = jnp.float32
BF16 = jnp.bfloat16
MESH = pl.DeviceIdType.MESH


def mm(a, b):
    return jnp.dot(a, b, preferred_element_type=F32)


def fold(x, op):
    return op(x.reshape(x.shape[0] // 8, 8, x.shape[1]), axis=0)


def flip(x):
    return jnp.concatenate([x[:, h * HEAD : (h + 1) * HEAD].T for h in range(GROUP)], axis=1)


def stack(x):
    return jnp.concatenate([x[:, h * HEAD : (h + 1) * HEAD] for h in range(GROUP)], axis=0)


def attend(base, bias, q, g, k_win, v_win, k_flip, v_flip, k_sum, v_sum, s_buf, p_buf, d_buf):
    q_flip, q_rows = flip(q), stack(q)
    count = WIN * TILE // CHUNK
    per = CHUNK // TILE
    top = jnp.full((8, COLS), LOW, F32)
    for c in range(count):
        s = mm(k_win[pl.ds(base + c * CHUNK, CHUNK), :], q_flip)
        if c == count - 1:
            key = lax.broadcasted_iota(jnp.int32, (TILE, COLS), 0)
            tok = lax.broadcasted_iota(jnp.int32, (TILE, COLS), 1) % TILE
            last = jnp.where(key <= tok, s[CHUNK - TILE :], LOW)
            s = jnp.concatenate([s[: CHUNK - TILE], last], axis=0)
        s_buf[c * CHUNK : (c + 1) * CHUNK, :] = s
        for u in range(per):
            top = jnp.maximum(top, fold(s[u * TILE : (u + 1) * TILE], jnp.max) + bias[c * per + u])
    top = jnp.max(top, axis=0, keepdims=True)
    total = jnp.zeros((8, COLS), F32)
    for c in range(WIN):
        rows = slice(c * TILE, (c + 1) * TILE)
        p = jnp.exp2((s_buf[rows, :] - (top - bias[c])) * SCALE)
        total = total + fold(p, jnp.sum)
        p_buf[rows, :] = p.astype(BF16)
    inverse = 1.0 / jnp.sum(total, axis=0, keepdims=True)
    out = (mm(v_flip[:, pl.ds(base, WIN * TILE)], p_buf[...]) * inverse).astype(BF16)
    g_flip = (flip(g).astype(F32) * inverse).astype(BF16)
    g_rows = stack(flip(g_flip))
    delta = jnp.sum(g_flip.astype(F32) * out.astype(F32), axis=0, keepdims=True)
    for c in range(count):
        rows = slice(c * CHUNK, (c + 1) * CHUNK)
        keys = pl.ds(base + c * CHUNK, CHUNK)
        p = p_buf[rows, :]
        d_prob = mm(v_win[keys, :], g_flip)
        d_score = (p.astype(F32) * (d_prob - delta)).astype(BF16)
        d_buf[rows, :] = d_score
        v_sum[keys, :] += mm(p, g_rows)
        k_sum[keys, :] += mm(d_score, q_rows)
    d_query = (mm(k_flip[:, pl.ds(base, WIN * TILE)], d_buf[...]) * FACTOR).astype(BF16)
    return flip(out), flip(d_query)


ORDER = (
    (6, 3, 0, 1, 2, 7, 4, 5),
    (7, 3, 0, 1, 2, 6, 4, 5),
    (4, 3, 2, 0, 1, 5, 6, 7),
    (5, 3, 2, 1, 0, 4, 6, 7),
    (6, 4, 5, 2, 3, 0, 1, 7),
    (7, 5, 4, 3, 2, 0, 1, 6),
    (6, 7, 4, 0, 1, 2, 3, 5),
    (7, 6, 5, 1, 0, 2, 3, 4),
)
PIECES = ((SHARD - 3 * TILE, 3 * TILE), (SHARD - 5 * TILE, 2 * TILE), (0, 3 * TILE))
CODE = [sum(tile * 8**n for n, tile in enumerate(row)) for row in ORDER]
FIRST_MID = [min(n for n, t in enumerate(row) if t < 6) for row in ORDER]
FIRST_FAR = [min(n for n, t in enumerate(row) if t < 3) for row in ORDER]
LAST_FAR = [max(n for n, t in enumerate(row) if t < 3) for row in ORDER]
LAST_MID = [max(n for n, t in enumerate(row) if t < 6) for row in ORDER]


def by_head(h, values):
    result = jnp.int32(values[0])
    for n in range(1, 8):
        result = jnp.where(h == n, values[n], result)
    return result


def kernel(
    seqs, starts_in, q_in, k_in, v_in, g_in, o_out, dq_out, dk_out, dv_out,
    starts, q_buf, g_buf, o_buf, dq_buf, k_win, v_win, k_flip, v_flip, k_sum, v_sum, s_buf, p_buf, d_buf,
    k_part, v_part, k_near, v_near, k_far, v_far,
    in_send, q_recv, g_recv, out_send, o_recv, dq_recv, z_send, z_recv,
):
    s, h = lax.axis_index("seq"), lax.axis_index("head")
    x, core = h // 2, h % 2
    has_next, has_prev = s < seqs - 1, s > 0
    after, before = (lax.rem(s + 1, seqs), h), (lax.rem(s + seqs - 1, seqs), h)

    def head_of(dx, dc):
        return ((x + dx) % 4) * 2 + (core + dc) % 2

    own = [
        pltpu.make_async_copy(starts_in, starts, z_recv.at[18]),
        pltpu.make_async_copy(k_in, k_win.at[pl.ds(BACK, SHARD)], z_recv.at[16]),
        pltpu.make_async_copy(v_in, v_win.at[pl.ds(BACK, SHARD)], z_recv.at[17]),
    ]
    for copy in own:
        copy.start()
    barrier = pltpu.get_barrier_semaphore()
    others = [(s, head_of(dx, dc)) for dx in range(4) for dc in range(2) if dx or dc]
    for other in others:
        pl.semaphore_signal(barrier, inc=1, device_id=other, device_id_type=MESH)

    @pl.when(has_next)
    def _():
        pl.semaphore_signal(barrier, inc=1, device_id=after, device_id_type=MESH)

    @pl.when(has_prev)
    def _():
        pl.semaphore_signal(barrier, inc=1, device_id=before, device_id_type=MESH)

    pl.semaphore_wait(barrier, len(others) + jnp.where(has_next, 1, 0) + jnp.where(has_prev, 1, 0))

    def cols(head):
        return pl.ds(pl.multiple_of(head * COLS, COLS), COLS)

    def remote(src, dst, send_sem, recv_sem, to):
        return pltpu.make_async_remote_copy(
            src_ref=src, dst_ref=dst, send_sem=send_sem, recv_sem=recv_sem, device_id=to, device_id_type=MESH
        )

    def start(copies):
        for copy in copies:
            copy.start()

    def took(copies):
        for copy in copies:
            copy.wait_recv()

    def gone(copies):
        for copy in copies:
            copy.wait_send()

    def regroup(n, dx, dc):
        to = head_of(dx, dc)
        copies = [
            remote(q_in.at[:, cols(to)], q_buf.at[h], in_send.at[2 * n], q_recv.at[h], (s, to)),
            remote(g_in.at[:, cols(to)], g_buf.at[h], in_send.at[2 * n + 1], g_recv.at[h], (s, to)),
        ]
        start(copies)
        return copies

    def shift(n, first, size):
        return [
            remote(src.at[pl.ds(first, size)], dst.at[pl.ds(FAR + first, size)], z_send.at[n + m], z_recv.at[n + m], after)
            for m, (src, dst) in enumerate(((k_in, k_win), (v_in, v_win)))
        ]

    near_in = [shift(2 * n, *piece) for n, piece in enumerate(PIECES)]
    far_in = [
        remote(win.at[pl.ds(BACK - FAR, FAR)], win.at[pl.ds(0, FAR)], z_send.at[6 + m], z_recv.at[6 + m], after)
        for m, win in enumerate((k_win, v_win))
    ]

    @pl.when(has_next)
    def _():
        start(near_in[0])

    first_ins = regroup(0, 1, 0) + regroup(1, 3, 0)

    @pl.when(has_next)
    def _():
        start(near_in[1])
        start(near_in[2])

    ins = regroup(2, 0, 1) + regroup(3, 1, 1) + regroup(4, 3, 1)
    start(
        [
            pltpu.make_async_copy(q_in.at[:, cols(h)], q_buf.at[h], q_recv.at[h]),
            pltpu.make_async_copy(g_in.at[:, cols(h)], g_buf.at[h], g_recv.at[h]),
        ]
    )

    def rows(j):
        return pl.ds(pl.multiple_of(j * TILE, TILE), TILE)

    def turn(j, carry):
        k_flip[:, rows(j)] = k_win[rows(j), :].T
        v_flip[:, rows(j)] = v_win[rows(j), :].T
        return carry

    def turn_piece(first, size):
        lax.fori_loop((FAR + first) // TILE, (FAR + first + size) // TILE, turn, 0)

    k_sum[...] = jnp.zeros_like(k_sum)
    v_sum[...] = jnp.zeros_like(v_sum)

    @pl.when(jnp.logical_not(has_prev))
    def _():
        for win in (k_win, v_win):
            win[0:BACK, :] = jnp.zeros((BACK, HEAD), BF16)

    @pl.when(jnp.logical_not(has_next))
    def _():
        for buf in (k_near, v_near, k_far, v_far):
            buf[...] = jnp.zeros_like(buf)

    for copy in own:
        copy.wait()
    lax.fori_loop(BACK // TILE, ROWS // TILE, turn, 0)

    @pl.when(has_prev)
    def _():
        took(near_in[0])

    @pl.when(has_next)
    def _():
        start(far_in)

    turn_piece(*PIECES[0])
    gone(first_ins)
    ins += regroup(5, 2, 0) + regroup(6, 2, 1)

    @pl.when(has_prev)
    def _():
        took(near_in[1])

    turn_piece(*PIECES[1])

    def arrived(buf, i, sem):
        pltpu.make_async_copy(buf.at[i], buf.at[i], sem.at[i]).wait()

    code = by_head(h, CODE)
    first_mid, first_far = by_head(h, FIRST_MID), by_head(h, FIRST_FAR)
    last_mid, last_far = by_head(h, LAST_MID), by_head(h, LAST_FAR)

    def to_part(j, carry):
        k_part[rows(j), :] = k_sum[rows(j), :].astype(BF16)
        v_part[rows(j), :] = v_sum[rows(j), :].astype(BF16)
        return carry

    parts = ((k_part, k_near, k_far), (v_part, v_near, v_far))
    far_back = [
        remote(part.at[pl.ds(0, FAR)], far, z_send.at[8 + m], z_recv.at[8 + m], before)
        for m, (part, near, far) in enumerate(parts)
    ]
    near_back = [
        [
            remote(
                part.at[pl.ds(FAR + first, size)], near.at[pl.ds(first, size)], z_send.at[10 + 2 * n + m],
                z_recv.at[10 + 2 * n + m] if n < 2 else z_recv.at[17 + 2 + m], before,
            )
            for m, (part, near, far) in enumerate(parts)
        ]
        for n, (first, size) in enumerate(PIECES[::-1])
    ]

    def step(r, left):
        i = left % 8
        tile = s * TILES + i
        begin = jnp.int32(0)
        for n in range(starts.shape[0]):
            begin = jnp.maximum(begin, jnp.where(starts[n] <= tile * TILE, starts[n], 0))
        bias = [jnp.where((tile - REACH + c) * TILE >= begin, 0.0, LOW).astype(F32) for c in range(WIN)]

        @pl.when(r == first_mid)
        def _():
            @pl.when(has_prev)
            def _():
                took(near_in[2])

            turn_piece(*PIECES[2])

        @pl.when(r == first_far)
        def _():
            @pl.when(has_prev)
            def _():
                took(far_in)

            lax.fori_loop(0, FAR // TILE, turn, 0)

        arrived(q_buf, i, q_recv)
        arrived(g_buf, i, g_recv)
        out, d_query = attend(
            pl.multiple_of(i * TILE, TILE), bias, q_buf[i], g_buf[i], k_win, v_win, k_flip, v_flip, k_sum, v_sum,
            s_buf, p_buf, d_buf,
        )
        o_buf[i] = out
        dq_buf[i] = d_query

        @pl.when(i == h)
        def _():
            start(
                [
                    pltpu.make_async_copy(o_buf.at[i], o_out.at[:, cols(h)], o_recv.at[h]),
                    pltpu.make_async_copy(dq_buf.at[i], dq_out.at[:, cols(h)], dq_recv.at[h]),
                ]
            )

        @pl.when(i != h)
        def _():
            start(
                [
                    remote(o_buf.at[i], o_out.at[:, cols(h)], out_send.at[2 * r], o_recv.at[h], (s, i)),
                    remote(dq_buf.at[i], dq_out.at[:, cols(h)], out_send.at[2 * r + 1], dq_recv.at[h], (s, i)),
                ]
            )

        @pl.when(r == last_far)
        def _():
            lax.fori_loop(0, FAR // TILE, to_part, 0)

            @pl.when(has_prev)
            def _():
                start(far_back)

        @pl.when(r == last_mid)
        def _():
            lax.fori_loop(FAR // TILE, FAR // TILE + 3, to_part, 0)

            @pl.when(has_prev)
            def _():
                start(near_back[0])

        return left // 8

    lax.fori_loop(0, 8, step, code)

    lax.fori_loop(FAR // TILE + 3, FAR // TILE + 5, to_part, 0)

    @pl.when(has_prev)
    def _():
        start(near_back[1])

    @pl.when(has_next)
    def _():
        took(far_back)

    def to_part_far(j, carry):
        full = rows(BACK // TILE - 3 + j)
        k_part[full, :] = (k_sum[full, :] + k_far[rows(j), :].astype(F32)).astype(BF16)
        v_part[full, :] = (v_sum[full, :] + v_far[rows(j), :].astype(F32)).astype(BF16)
        return carry

    lax.fori_loop(0, 3, to_part_far, 0)

    @pl.when(has_prev)
    def _():
        start(near_back[2])

    def total(j, carry):
        full = rows(BACK // TILE + j)
        dk_out[rows(j), :] = ((k_sum[full, :] + k_near[rows(j), :].astype(F32)) * FACTOR).astype(BF16)
        dv_out[rows(j), :] = (v_sum[full, :] + v_near[rows(j), :].astype(F32)).astype(BF16)
        return carry

    for n, (first, size) in enumerate(PIECES[::-1]):

        @pl.when(has_next)
        def _():
            took(near_back[n])

        lax.fori_loop(first // TILE, (first + size) // TILE, total, 0)

    gone(ins)

    @pl.when(has_next)
    def _():
        for copies in near_in + [far_in]:
            gone(copies)

    @pl.when(has_prev)
    def _():
        for copies in near_back + [far_back]:
            gone(copies)

    def finish(r, left):
        i = left % 8
        arrived(o_buf, i, o_recv)
        arrived(dq_buf, i, dq_recv)

        @pl.when(i != h)
        def _():
            for n in range(2):
                pltpu.make_async_copy(o_buf.at[i], o_buf.at[i], out_send.at[2 * r + n]).wait()

        return left // 8

    lax.fori_loop(0, 8, finish, code)


def local(seqs, queries, key_heads, value_heads, output_grad, doc_starts):
    vmem = pl.BlockSpec(memory_space=pltpu.VMEM)
    hbm = pl.BlockSpec(memory_space=pltpu.HBM)
    anywhere = pl.BlockSpec(memory_space=pl.ANY)
    dma = pltpu.SemaphoreType.DMA
    shapes = [jax.ShapeDtypeStruct(queries.shape, BF16)] * 2 + [jax.ShapeDtypeStruct(key_heads.shape, BF16)] * 2
    results = pl.pallas_call(
        functools.partial(kernel, seqs),
        out_shape=shapes,
        in_specs=[hbm] * 5,
        out_specs=[anywhere, anywhere, vmem, vmem],
        scratch_shapes=[pltpu.SMEM(doc_starts.shape, jnp.int32)]
        + [pltpu.VMEM((TILES, TILE, COLS), BF16)] * 4
        + [pltpu.VMEM((ROWS, HEAD), BF16)] * 2
        + [pltpu.VMEM((HEAD, ROWS), BF16)] * 2
        + [pltpu.VMEM((ROWS, HEAD), F32)] * 2
        + [pltpu.VMEM((WIN * TILE, COLS), F32)]
        + [pltpu.VMEM((WIN * TILE, COLS), BF16)] * 2
        + [pltpu.VMEM((BACK, HEAD), BF16)] * 2
        + [pltpu.VMEM((NEAR, HEAD), BF16)] * 2
        + [pltpu.VMEM((FAR, HEAD), BF16)] * 2
        + [dma((14,)), dma((8,)), dma((8,)), dma((16,)), dma((8,)), dma((8,)), dma((16,)), dma((21,))],
        compiler_params=pltpu.CompilerParams(
            collective_id=0, has_side_effects=True, vmem_limit_bytes=48 << 20
        ),
        cost_estimate=pl.CostEstimate(flops=10**10, bytes_accessed=8 << 20, transcendentals=6 << 20),
        name="attention",
    )(*(pltpu.with_memory_space_constraint(a, pltpu.HBM) for a in (doc_starts, queries, key_heads, value_heads, output_grad)))
    return results


def solution(mesh):
    wide = P(("seq", "head"), None)
    narrow = P("seq", "head")
    return jax.shard_map(
        functools.partial(local, mesh.shape["seq"]),
        mesh=mesh,
        in_specs=(wide, narrow, narrow, wide, P()),
        out_specs=(wide, wide, narrow, narrow),
        check_vma=False,
    )
```

```python
import functools
import math

import jax
import jax.numpy as jnp
from jax import lax
from jax.experimental import pallas as pl
from jax.experimental.pallas import tpu as pltpu
from jax.sharding import PartitionSpec as P

HEAD = 128
QH = 32
KVH = 8
TILE = 128
SHARD = 1024
REACH = 11
WIN = REACH + 1
GROUP = QH // KVH
COLS = GROUP * HEAD
TILES = SHARD // TILE
NEAR = SHARD
FAR = REACH * TILE - SHARD
BACK = NEAR + FAR
ROWS = BACK + SHARD
CHUNK = 256
FACTOR = HEAD**-0.5
SCALE = FACTOR * math.log2(math.e)
LOW = -1e30
F32 = jnp.float32
BF16 = jnp.bfloat16
MESH = pl.DeviceIdType.MESH


def mm(a, b):
    return jnp.dot(a, b, preferred_element_type=F32)


def mm_rows(a, b):
    return lax.dot_general(a, b, (((1,), (1,)), ((), ())), preferred_element_type=F32)


def fold(x, op):
    return op(x.reshape(x.shape[0] // 8, 8, x.shape[1]), axis=0)


def flip(x):
    return jnp.concatenate([x[:, h * HEAD : (h + 1) * HEAD].T for h in range(GROUP)], axis=1)


def stack(x):
    return jnp.concatenate([x[:, h * HEAD : (h + 1) * HEAD] for h in range(GROUP)], axis=0)


def attend(base, bias, q, g, k_win, v_win, k_flip, v_flip, k_sum, v_sum, s_buf, p_buf, d_buf):
    q_rows = stack(q)
    count = WIN * TILE // CHUNK
    per = CHUNK // TILE
    top = jnp.full((8, COLS), LOW, F32)
    for c in range(count):
        s = mm_rows(k_win[pl.ds(base + c * CHUNK, CHUNK), :], q_rows)
        if c == count - 1:
            key = lax.broadcasted_iota(jnp.int32, (TILE, COLS), 0)
            tok = lax.broadcasted_iota(jnp.int32, (TILE, COLS), 1) % TILE
            last = jnp.where(key <= tok, s[CHUNK - TILE :], LOW)
            s = jnp.concatenate([s[: CHUNK - TILE], last], axis=0)
        s_buf[c * CHUNK : (c + 1) * CHUNK, :] = s
        for u in range(per):
            top = jnp.maximum(top, fold(s[u * TILE : (u + 1) * TILE], jnp.max) + bias[c * per + u])
    top = jnp.max(top, axis=0, keepdims=True)
    total = jnp.zeros((8, COLS), F32)
    for c in range(WIN):
        rows = slice(c * TILE, (c + 1) * TILE)
        p = jnp.exp2((s_buf[rows, :] - (top - bias[c])) * SCALE)
        total = total + fold(p, jnp.sum)
        p_buf[rows, :] = p.astype(BF16)
    inverse = 1.0 / jnp.sum(total, axis=0, keepdims=True)
    out = (mm(v_flip[:, pl.ds(base, WIN * TILE)], p_buf[...]) * inverse).astype(BF16)
    g_flip = (flip(g).astype(F32) * inverse).astype(BF16)
    delta = jnp.sum(g_flip.astype(F32) * out.astype(F32), axis=0, keepdims=True)
    for c in range(count):
        rows = slice(c * CHUNK, (c + 1) * CHUNK)
        keys = pl.ds(base + c * CHUNK, CHUNK)
        p = p_buf[rows, :]
        d_prob = mm(v_win[keys, :], g_flip)
        d_score = p * (d_prob - delta).astype(BF16)
        d_buf[rows, :] = d_score
        v_sum[keys, :] += mm_rows(p, g_flip)
        k_sum[keys, :] += mm(d_score, q_rows)
    d_query = (mm(k_flip[:, pl.ds(base, WIN * TILE)], d_buf[...]) * FACTOR).astype(BF16)
    return flip(out), flip(d_query)


ORDER = (
    (6, 3, 0, 1, 2, 7, 4, 5),
    (7, 3, 0, 1, 2, 6, 4, 5),
    (4, 3, 2, 0, 1, 5, 6, 7),
    (5, 3, 2, 1, 0, 4, 6, 7),
    (6, 4, 5, 2, 3, 0, 1, 7),
    (7, 5, 4, 3, 2, 0, 1, 6),
    (6, 7, 4, 0, 1, 2, 3, 5),
    (7, 6, 4, 1, 0, 2, 3, 5),
)

PIECES = ((SHARD - 3 * TILE, 3 * TILE), (SHARD - 5 * TILE, 2 * TILE), (0, 3 * TILE))
CODE = [sum(tile * 8**n for n, tile in enumerate(row)) for row in ORDER]
FIRST_MID = [min(n for n, t in enumerate(row) if t < 6) for row in ORDER]
FIRST_FAR = [min(n for n, t in enumerate(row) if t < 3) for row in ORDER]
LAST_FAR = [max(n for n, t in enumerate(row) if t < 3) for row in ORDER]
BACK_PIECES = ((0, 2 * TILE), (2 * TILE, 6 * TILE))
LAST_MID = [max(n for n, t in enumerate(row) if t < 5) for row in ORDER]


def by_head(h, values):
    result = jnp.int32(values[0])
    for n in range(1, 8):
        result = jnp.where(h == n, values[n], result)
    return result


def kernel(
    seqs, starts_in, q_in, k_in, v_in, g_in, o_out, dq_out, dk_out, dv_out,
    starts, q_buf, g_buf, o_buf, dq_buf, k_win, v_win, k_flip, v_flip, k_sum, v_sum, s_buf, p_buf, d_buf,
    k_part, v_part, k_near, v_near, k_far, v_far,
    in_send, q_recv, g_recv, out_send, o_recv, dq_recv, z_send, z_recv,
):
    s, h = lax.axis_index("seq"), lax.axis_index("head")
    x, core = h // 2, h % 2
    has_next, has_prev = s < seqs - 1, s > 0
    after, before = (lax.rem(s + 1, seqs), h), (lax.rem(s + seqs - 1, seqs), h)

    def head_of(dx, dc):
        return ((x + dx) % 4) * 2 + (core + dc) % 2

    own = [
        pltpu.make_async_copy(starts_in, starts, z_recv.at[18]),
        pltpu.make_async_copy(k_in, k_win.at[pl.ds(BACK, SHARD)], z_recv.at[16]),
        pltpu.make_async_copy(v_in, v_win.at[pl.ds(BACK, SHARD)], z_recv.at[17]),
    ]
    for copy in own:
        copy.start()
    barrier = pltpu.get_barrier_semaphore()
    others = [(s, head_of(dx, dc)) for dx in range(4) for dc in range(2) if dx or dc]
    for other in others:
        pl.semaphore_signal(barrier, inc=1, device_id=other, device_id_type=MESH)

    @pl.when(has_prev)
    def _():
        pl.semaphore_signal(barrier, inc=1, device_id=before, device_id_type=MESH)

    pl.semaphore_wait(barrier, len(others) + jnp.where(has_next, 1, 0))

    def cols(head):
        return pl.ds(pl.multiple_of(head * COLS, COLS), COLS)

    def remote(src, dst, send_sem, recv_sem, to):
        return pltpu.make_async_remote_copy(
            src_ref=src, dst_ref=dst, send_sem=send_sem, recv_sem=recv_sem, device_id=to, device_id_type=MESH
        )

    def start(copies):
        for copy in copies:
            copy.start()

    def took(copies):
        for copy in copies:
            copy.wait_recv()

    def gone(copies):
        for copy in copies:
            copy.wait_send()

    def regroup(n, dx, dc):
        to = head_of(dx, dc)
        copies = [
            remote(q_in.at[:, cols(to)], q_buf.at[h], in_send.at[2 * n], q_recv.at[h], (s, to)),
            remote(g_in.at[:, cols(to)], g_buf.at[h], in_send.at[2 * n + 1], g_recv.at[h], (s, to)),
        ]
        start(copies)
        return copies

    def shift(n, first, size):
        return [
            remote(src.at[pl.ds(first, size)], dst.at[pl.ds(FAR + first, size)], z_send.at[n + m], z_recv.at[n + m], after)
            for m, (src, dst) in enumerate(((k_in, k_win), (v_in, v_win)))
        ]

    near_in = [shift(2 * n, *piece) for n, piece in enumerate(PIECES)]
    far_in = [
        remote(win.at[pl.ds(BACK - FAR, FAR)], win.at[pl.ds(0, FAR)], z_send.at[6 + m], z_recv.at[6 + m], after)
        for m, win in enumerate((k_win, v_win))
    ]

    @pl.when(has_next)
    def _():
        for copies in near_in:
            start(copies)

    first_ins = regroup(0, 1, 0) + regroup(1, 3, 0)

    ins = regroup(2, 0, 1) + regroup(3, 1, 1) + regroup(4, 3, 1)
    start(
        [
            pltpu.make_async_copy(q_in.at[:, cols(h)], q_buf.at[h], q_recv.at[h]),
            pltpu.make_async_copy(g_in.at[:, cols(h)], g_buf.at[h], g_recv.at[h]),
        ]
    )

    def rows(j):
        return pl.ds(pl.multiple_of(j * TILE, TILE), TILE)

    def turn(j, carry):
        k_flip[:, rows(j)] = k_win[rows(j), :].T
        v_flip[:, rows(j)] = v_win[rows(j), :].T
        return carry

    def turn_piece(first, size):
        lax.fori_loop((FAR + first) // TILE, (FAR + first + size) // TILE, turn, 0)

    k_sum[...] = jnp.zeros_like(k_sum)
    v_sum[...] = jnp.zeros_like(v_sum)

    @pl.when(jnp.logical_not(has_prev))
    def _():
        for win in (k_win, v_win):
            win[0:BACK, :] = jnp.zeros((BACK, HEAD), BF16)

    @pl.when(jnp.logical_not(has_next))
    def _():
        for buf in (k_near, v_near, k_far, v_far):
            buf[...] = jnp.zeros_like(buf)

    for copy in own:
        copy.wait()
    lax.fori_loop(BACK // TILE, ROWS // TILE, turn, 0)

    @pl.when(has_prev)
    def _():
        took(near_in[0])

    @pl.when(has_next)
    def _():
        start(far_in)

    turn_piece(*PIECES[0])
    gone(first_ins)
    ins += regroup(5, 2, 0) + regroup(6, 2, 1)

    @pl.when(has_prev)
    def _():
        took(near_in[1])

    turn_piece(*PIECES[1])

    def arrived(buf, i, sem):
        pltpu.make_async_copy(buf.at[i], buf.at[i], sem.at[i]).wait()

    code = by_head(h, CODE)
    first_mid, first_far = by_head(h, FIRST_MID), by_head(h, FIRST_FAR)
    last_mid, last_far = by_head(h, LAST_MID), by_head(h, LAST_FAR)

    def to_part(j, carry):
        k_part[rows(j), :] = k_sum[rows(j), :].astype(BF16)
        v_part[rows(j), :] = v_sum[rows(j), :].astype(BF16)
        return carry

    parts = ((k_part, k_near, k_far), (v_part, v_near, v_far))
    far_back = [
        remote(part.at[pl.ds(0, FAR)], far, z_send.at[8 + m], z_recv.at[8 + m], before)
        for m, (part, near, far) in enumerate(parts)
    ]
    near_back = [
        [
            remote(
                part.at[pl.ds(FAR + first, size)], near.at[pl.ds(first, size)], z_send.at[10 + 2 * n + m],
                z_recv.at[10 + 2 * n + m], before,
            )
            for m, (part, near, far) in enumerate(parts)
        ]
        for n, (first, size) in enumerate(BACK_PIECES)
    ]

    def step(r, left):
        i = left % 8
        tile = s * TILES + i
        begin = jnp.int32(0)
        for n in range(starts.shape[0]):
            begin = jnp.maximum(begin, jnp.where(starts[n] <= tile * TILE, starts[n], 0))
        bias = [jnp.where((tile - REACH + c) * TILE >= begin, 0.0, LOW).astype(F32) for c in range(WIN)]

        @pl.when(r == first_mid)
        def _():
            @pl.when(has_prev)
            def _():
                took(near_in[2])

            turn_piece(*PIECES[2])

        @pl.when(r == first_far)
        def _():
            @pl.when(has_prev)
            def _():
                took(far_in)

            lax.fori_loop(0, FAR // TILE, turn, 0)

        arrived(q_buf, i, q_recv)
        arrived(g_buf, i, g_recv)
        out, d_query = attend(
            pl.multiple_of(i * TILE, TILE), bias, q_buf[i], g_buf[i], k_win, v_win, k_flip, v_flip, k_sum, v_sum,
            s_buf, p_buf, d_buf,
        )
        o_buf[i] = out
        dq_buf[i] = d_query

        @pl.when(i == h)
        def _():
            start(
                [
                    pltpu.make_async_copy(o_buf.at[i], o_out.at[:, cols(h)], o_recv.at[h]),
                    pltpu.make_async_copy(dq_buf.at[i], dq_out.at[:, cols(h)], dq_recv.at[h]),
                ]
            )

        @pl.when(i != h)
        def _():
            start(
                [
                    remote(o_buf.at[i], o_out.at[:, cols(h)], out_send.at[2 * r], o_recv.at[h], (s, i)),
                    remote(dq_buf.at[i], dq_out.at[:, cols(h)], out_send.at[2 * r + 1], dq_recv.at[h], (s, i)),
                ]
            )

        @pl.when(r == last_far)
        def _():
            lax.fori_loop(0, FAR // TILE, to_part, 0)

            @pl.when(has_prev)
            def _():
                start(far_back)

        @pl.when(r == last_mid)
        def _():
            lax.fori_loop(FAR // TILE, FAR // TILE + 2, to_part, 0)

            @pl.when(has_prev)
            def _():
                start(near_back[0])

        return left // 8

    lax.fori_loop(0, 8, step, code)

    lax.fori_loop(FAR // TILE + 2, FAR // TILE + 5, to_part, 0)

    @pl.when(has_next)
    def _():
        took(far_back)

    def to_part_far(j, carry):
        full = rows(BACK // TILE - 3 + j)
        k_part[full, :] = (k_sum[full, :] + k_far[rows(j), :].astype(F32)).astype(BF16)
        v_part[full, :] = (v_sum[full, :] + v_far[rows(j), :].astype(F32)).astype(BF16)
        return carry

    lax.fori_loop(0, 3, to_part_far, 0)

    @pl.when(has_prev)
    def _():
        start(near_back[1])

    def total(j, carry):
        full = rows(BACK // TILE + j)
        dk_out[rows(j), :] = ((k_sum[full, :] + k_near[rows(j), :].astype(F32)) * FACTOR).astype(BF16)
        dv_out[rows(j), :] = (v_sum[full, :] + v_near[rows(j), :].astype(F32)).astype(BF16)
        return carry

    for n, (first, size) in enumerate(BACK_PIECES):

        @pl.when(has_next)
        def _():
            took(near_back[n])

        lax.fori_loop(first // TILE, (first + size) // TILE, total, 0)

    gone(ins)

    @pl.when(has_next)
    def _():
        for copies in near_in + [far_in]:
            gone(copies)

    @pl.when(has_prev)
    def _():
        for copies in near_back + [far_back]:
            gone(copies)

    def finish(r, left):
        i = left % 8
        arrived(o_buf, i, o_recv)
        arrived(dq_buf, i, dq_recv)

        @pl.when(i != h)
        def _():
            for n in range(2):
                pltpu.make_async_copy(o_buf.at[i], o_buf.at[i], out_send.at[2 * r + n]).wait()

        return left // 8

    lax.fori_loop(0, 8, finish, code)


def local(seqs, queries, key_heads, value_heads, output_grad, doc_starts):
    vmem = pl.BlockSpec(memory_space=pltpu.VMEM)
    hbm = pl.BlockSpec(memory_space=pltpu.HBM)
    anywhere = pl.BlockSpec(memory_space=pl.ANY)
    dma = pltpu.SemaphoreType.DMA
    shapes = [jax.ShapeDtypeStruct(queries.shape, BF16)] * 2 + [jax.ShapeDtypeStruct(key_heads.shape, BF16)] * 2
    results = pl.pallas_call(
        functools.partial(kernel, seqs),
        out_shape=shapes,
        in_specs=[hbm] * 5,
        out_specs=[anywhere, anywhere, vmem, vmem],
        scratch_shapes=[pltpu.SMEM(doc_starts.shape, jnp.int32)]
        + [pltpu.VMEM((TILES, TILE, COLS), BF16)] * 4
        + [pltpu.VMEM((ROWS, HEAD), BF16)] * 2
        + [pltpu.VMEM((HEAD, ROWS), BF16)] * 2
        + [pltpu.VMEM((ROWS, HEAD), F32)] * 2
        + [pltpu.VMEM((WIN * TILE, COLS), F32)]
        + [pltpu.VMEM((WIN * TILE, COLS), BF16)] * 2
        + [pltpu.VMEM((BACK, HEAD), BF16)] * 2
        + [pltpu.VMEM((NEAR, HEAD), BF16)] * 2
        + [pltpu.VMEM((FAR, HEAD), BF16)] * 2
        + [dma((14,)), dma((8,)), dma((8,)), dma((16,)), dma((8,)), dma((8,)), dma((14,)), dma((19,))],
        compiler_params=pltpu.CompilerParams(
            collective_id=0, has_side_effects=True, vmem_limit_bytes=48 << 20
        ),
        cost_estimate=pl.CostEstimate(flops=10**10, bytes_accessed=8 << 20, transcendentals=6 << 20),
        name="attention",
    )(*(pltpu.with_memory_space_constraint(a, pltpu.HBM) for a in (doc_starts, queries, key_heads, value_heads, output_grad)))
    return results


def solution(mesh):
    wide = P(("seq", "head"), None)
    narrow = P("seq", "head")
    return jax.shard_map(
        functools.partial(local, mesh.shape["seq"]),
        mesh=mesh,
        in_specs=(wide, narrow, narrow, wide, P()),
        out_specs=(wide, wide, narrow, narrow),
        check_vma=False,
    )
```

```python
import functools
import math

import jax
import jax.numpy as jnp
from jax import lax
from jax.experimental import pallas as pl
from jax.experimental.pallas import tpu as pltpu
from jax.sharding import PartitionSpec as P

HEAD = 128
QH = 32
KVH = 8
TILE = 128
SHARD = 1024
REACH = 11
WIN = REACH + 1
GROUP = QH // KVH
COLS = GROUP * HEAD
TILES = SHARD // TILE
NEAR = SHARD
FAR = REACH * TILE - SHARD
BACK = NEAR + FAR
ROWS = BACK + SHARD
CHUNK = 256
FACTOR = HEAD**-0.5
SCALE = FACTOR * math.log2(math.e)
LOW = -1e30
F32 = jnp.float32
BF16 = jnp.bfloat16
MESH = pl.DeviceIdType.MESH


def mm(a, b):
    return jnp.dot(a, b, preferred_element_type=F32)


def mm_rows(a, b):
    return lax.dot_general(a, b, (((1,), (1,)), ((), ())), preferred_element_type=F32)


def fold(x, op):
    return op(x.reshape(x.shape[0] // 8, 8, x.shape[1]), axis=0)


def flip(x):
    return jnp.concatenate([x[:, h * HEAD : (h + 1) * HEAD].T for h in range(GROUP)], axis=1)


def stack(x):
    return jnp.concatenate([x[:, h * HEAD : (h + 1) * HEAD] for h in range(GROUP)], axis=0)


def attend(base, bias, q, g, k_win, v_win, k_flip, v_flip, k_sum, v_sum, s_buf, p_buf, d_buf):
    q_rows = stack(q)
    count = WIN * TILE // CHUNK
    per = CHUNK // TILE
    top = jnp.full((8, COLS), LOW, F32)
    for c in range(count):
        s = mm_rows(k_win[pl.ds(base + c * CHUNK, CHUNK), :], q_rows)
        if c == count - 1:
            key = lax.broadcasted_iota(jnp.int32, (TILE, COLS), 0)
            tok = lax.broadcasted_iota(jnp.int32, (TILE, COLS), 1) % TILE
            last = jnp.where(key <= tok, s[CHUNK - TILE :], LOW)
            s = jnp.concatenate([s[: CHUNK - TILE], last], axis=0)
        s_buf[c * CHUNK : (c + 1) * CHUNK, :] = s
        for u in range(per):
            top = jnp.maximum(top, fold(s[u * TILE : (u + 1) * TILE], jnp.max) + bias[c * per + u])
    top = jnp.max(top, axis=0, keepdims=True)
    total = jnp.zeros((8, COLS), F32)
    for c in range(WIN):
        rows = slice(c * TILE, (c + 1) * TILE)
        p = jnp.exp2((s_buf[rows, :] - (top - bias[c])) * SCALE)
        total = total + fold(p, jnp.sum)
        p_buf[rows, :] = p.astype(BF16)
    inverse = 1.0 / jnp.sum(total, axis=0, keepdims=True)
    out = (mm(v_flip[:, pl.ds(base, WIN * TILE)], p_buf[...]) * inverse).astype(BF16)
    g_flip = (flip(g).astype(F32) * inverse).astype(BF16)
    delta = jnp.sum(g_flip.astype(F32) * out.astype(F32), axis=0, keepdims=True)
    for c in range(count):
        rows = slice(c * CHUNK, (c + 1) * CHUNK)
        keys = pl.ds(base + c * CHUNK, CHUNK)
        p = p_buf[rows, :]
        d_prob = mm(v_win[keys, :], g_flip)
        d_score = p * (d_prob - delta).astype(BF16)
        d_buf[rows, :] = d_score
        v_sum[keys, :] += mm_rows(p, g_flip)
        k_sum[keys, :] += mm(d_score, q_rows)
    d_query = (mm(k_flip[:, pl.ds(base, WIN * TILE)], d_buf[...]) * FACTOR).astype(BF16)
    return flip(out), flip(d_query)


ORDER = (
    (6, 3, 0, 1, 2, 7, 4, 5),
    (7, 3, 0, 1, 2, 6, 4, 5),
    (4, 3, 2, 0, 1, 5, 6, 7),
    (5, 3, 2, 1, 0, 4, 6, 7),
    (6, 4, 5, 2, 3, 0, 1, 7),
    (7, 5, 4, 3, 2, 0, 1, 6),
    (6, 7, 4, 0, 1, 2, 3, 5),
    (7, 6, 4, 1, 0, 2, 3, 5),
)

PIECES = ((SHARD - 3 * TILE, 3 * TILE), (SHARD - 6 * TILE, 3 * TILE), (0, 2 * TILE))
CODE = [sum(tile * 8**n for n, tile in enumerate(row)) for row in ORDER]
FIRST_MID = [min(n for n, t in enumerate(row) if t < 5) for row in ORDER]
FIRST_FAR = [min(n for n, t in enumerate(row) if t < 3) for row in ORDER]
LAST_FAR = [max(n for n, t in enumerate(row) if t < 3) for row in ORDER]
BACK_PIECES = ((0, 2 * TILE), (2 * TILE, 6 * TILE))
LAST_MID = [max(n for n, t in enumerate(row) if t < 5) for row in ORDER]


def by_head(h, values):
    result = jnp.int32(values[0])
    for n in range(1, 8):
        result = jnp.where(h == n, values[n], result)
    return result


def kernel(
    seqs, starts_in, q_in, k_in, v_in, g_in, o_out, dq_out, dk_out, dv_out,
    starts, q_buf, g_buf, o_buf, dq_buf, k_win, v_win, k_flip, v_flip, k_sum, v_sum, s_buf, p_buf, d_buf,
    k_part, v_part, k_near, v_near, k_far, v_far,
    in_send, q_recv, g_recv, out_send, o_recv, dq_recv, z_send, z_recv,
):
    s, h = lax.axis_index("seq"), lax.axis_index("head")
    x, core = h // 2, h % 2
    has_next, has_prev = s < seqs - 1, s > 0
    after, before = (lax.rem(s + 1, seqs), h), (lax.rem(s + seqs - 1, seqs), h)

    def head_of(dx, dc):
        return ((x + dx) % 4) * 2 + (core + dc) % 2

    own = [
        pltpu.make_async_copy(starts_in, starts, z_recv.at[18]),
        pltpu.make_async_copy(k_in, k_win.at[pl.ds(BACK, SHARD)], z_recv.at[16]),
        pltpu.make_async_copy(v_in, v_win.at[pl.ds(BACK, SHARD)], z_recv.at[17]),
    ]
    for copy in own:
        copy.start()
    barrier = pltpu.get_barrier_semaphore()
    others = [(s, head_of(dx, dc)) for dx in range(4) for dc in range(2) if dx or dc]
    for other in others:
        pl.semaphore_signal(barrier, inc=1, device_id=other, device_id_type=MESH)

    @pl.when(has_prev)
    def _():
        pl.semaphore_signal(barrier, inc=1, device_id=before, device_id_type=MESH)

    pl.semaphore_wait(barrier, len(others) + jnp.where(has_next, 1, 0))

    def cols(head):
        return pl.ds(pl.multiple_of(head * COLS, COLS), COLS)

    def remote(src, dst, send_sem, recv_sem, to):
        return pltpu.make_async_remote_copy(
            src_ref=src, dst_ref=dst, send_sem=send_sem, recv_sem=recv_sem, device_id=to, device_id_type=MESH
        )

    def start(copies):
        for copy in copies:
            copy.start()

    def took(copies):
        for copy in copies:
            copy.wait_recv()

    def gone(copies):
        for copy in copies:
            copy.wait_send()

    def regroup(n, dx, dc):
        to = head_of(dx, dc)
        copies = [
            remote(q_in.at[:, cols(to)], q_buf.at[h], in_send.at[2 * n], q_recv.at[h], (s, to)),
            remote(g_in.at[:, cols(to)], g_buf.at[h], in_send.at[2 * n + 1], g_recv.at[h], (s, to)),
        ]
        start(copies)
        return copies

    def shift(n, first, size):
        return [
            remote(src.at[pl.ds(first, size)], dst.at[pl.ds(FAR + first, size)], z_send.at[n + m], z_recv.at[n + m], after)
            for m, (src, dst) in enumerate(((k_in, k_win), (v_in, v_win)))
        ]

    near_in = [shift(2 * n, *piece) for n, piece in enumerate(PIECES)]
    far_in = [
        remote(win.at[pl.ds(BACK - FAR, FAR)], win.at[pl.ds(0, FAR)], z_send.at[6 + m], z_recv.at[6 + m], after)
        for m, win in enumerate((k_win, v_win))
    ]

    @pl.when(has_next)
    def _():
        for copies in near_in:
            start(copies)

    first_ins = regroup(0, 1, 0) + regroup(1, 3, 0)

    ins = regroup(2, 0, 1) + regroup(3, 1, 1) + regroup(4, 3, 1)
    start(
        [
            pltpu.make_async_copy(q_in.at[:, cols(h)], q_buf.at[h], q_recv.at[h]),
            pltpu.make_async_copy(g_in.at[:, cols(h)], g_buf.at[h], g_recv.at[h]),
        ]
    )

    def rows(j):
        return pl.ds(pl.multiple_of(j * TILE, TILE), TILE)

    def turn(j, carry):
        k_flip[:, rows(j)] = k_win[rows(j), :].T
        v_flip[:, rows(j)] = v_win[rows(j), :].T
        return carry

    def turn_piece(first, size):
        lax.fori_loop((FAR + first) // TILE, (FAR + first + size) // TILE, turn, 0)

    k_sum[...] = jnp.zeros_like(k_sum)
    v_sum[...] = jnp.zeros_like(v_sum)

    @pl.when(jnp.logical_not(has_prev))
    def _():
        for win in (k_win, v_win):
            win[0:BACK, :] = jnp.zeros((BACK, HEAD), BF16)

    @pl.when(jnp.logical_not(has_next))
    def _():
        for buf in (k_near, v_near, k_far, v_far):
            buf[...] = jnp.zeros_like(buf)

    for copy in own:
        copy.wait()
    lax.fori_loop(BACK // TILE, ROWS // TILE, turn, 0)

    @pl.when(has_prev)
    def _():
        took(near_in[0])

    @pl.when(has_next)
    def _():
        start(far_in)

    turn_piece(*PIECES[0])
    gone(first_ins)
    ins += regroup(5, 2, 0) + regroup(6, 2, 1)

    @pl.when(has_prev)
    def _():
        took(near_in[1])

    turn_piece(*PIECES[1])

    def arrived(buf, i, sem):
        pltpu.make_async_copy(buf.at[i], buf.at[i], sem.at[i]).wait()

    code = by_head(h, CODE)
    first_mid, first_far = by_head(h, FIRST_MID), by_head(h, FIRST_FAR)
    last_mid, last_far = by_head(h, LAST_MID), by_head(h, LAST_FAR)

    def to_part(j, carry):
        k_part[rows(j), :] = k_sum[rows(j), :].astype(BF16)
        v_part[rows(j), :] = v_sum[rows(j), :].astype(BF16)
        return carry

    parts = ((k_part, k_near, k_far), (v_part, v_near, v_far))
    far_back = [
        remote(part.at[pl.ds(0, FAR)], far, z_send.at[8 + m], z_recv.at[8 + m], before)
        for m, (part, near, far) in enumerate(parts)
    ]
    near_back = [
        [
            remote(
                part.at[pl.ds(FAR + first, size)], near.at[pl.ds(first, size)], z_send.at[10 + 2 * n + m],
                z_recv.at[10 + 2 * n + m], before,
            )
            for m, (part, near, far) in enumerate(parts)
        ]
        for n, (first, size) in enumerate(BACK_PIECES)
    ]

    def step(r, left):
        i = left % 8
        tile = s * TILES + i
        begin = jnp.int32(0)
        for n in range(starts.shape[0]):
            begin = jnp.maximum(begin, jnp.where(starts[n] <= tile * TILE, starts[n], 0))
        bias = [jnp.where((tile - REACH + c) * TILE >= begin, 0.0, LOW).astype(F32) for c in range(WIN)]

        @pl.when(r == first_mid)
        def _():
            @pl.when(has_prev)
            def _():
                took(near_in[2])

            turn_piece(*PIECES[2])

        @pl.when(r == first_far)
        def _():
            @pl.when(has_prev)
            def _():
                took(far_in)

            lax.fori_loop(0, FAR // TILE, turn, 0)

        arrived(q_buf, i, q_recv)
        arrived(g_buf, i, g_recv)
        out, d_query = attend(
            pl.multiple_of(i * TILE, TILE), bias, q_buf[i], g_buf[i], k_win, v_win, k_flip, v_flip, k_sum, v_sum,
            s_buf, p_buf, d_buf,
        )
        o_buf[i] = out
        dq_buf[i] = d_query

        @pl.when(i == h)
        def _():
            start(
                [
                    pltpu.make_async_copy(o_buf.at[i], o_out.at[:, cols(h)], o_recv.at[h]),
                    pltpu.make_async_copy(dq_buf.at[i], dq_out.at[:, cols(h)], dq_recv.at[h]),
                ]
            )

        @pl.when(i != h)
        def _():
            start(
                [
                    remote(o_buf.at[i], o_out.at[:, cols(h)], out_send.at[2 * r], o_recv.at[h], (s, i)),
                    remote(dq_buf.at[i], dq_out.at[:, cols(h)], out_send.at[2 * r + 1], dq_recv.at[h], (s, i)),
                ]
            )

        @pl.when(r == last_far)
        def _():
            lax.fori_loop(0, FAR // TILE, to_part, 0)

            @pl.when(has_prev)
            def _():
                start(far_back)

        @pl.when(r == last_mid)
        def _():
            lax.fori_loop(FAR // TILE, FAR // TILE + 2, to_part, 0)

            @pl.when(has_prev)
            def _():
                start(near_back[0])

        return left // 8

    lax.fori_loop(0, 8, step, code)

    lax.fori_loop(FAR // TILE + 2, FAR // TILE + 5, to_part, 0)

    @pl.when(has_next)
    def _():
        took(far_back)

    def to_part_far(j, carry):
        full = rows(BACK // TILE - 3 + j)
        k_part[full, :] = (k_sum[full, :] + k_far[rows(j), :].astype(F32)).astype(BF16)
        v_part[full, :] = (v_sum[full, :] + v_far[rows(j), :].astype(F32)).astype(BF16)
        return carry

    lax.fori_loop(0, 3, to_part_far, 0)

    @pl.when(has_prev)
    def _():
        start(near_back[1])

    def total(j, carry):
        full = rows(BACK // TILE + j)
        dk_out[rows(j), :] = ((k_sum[full, :] + k_near[rows(j), :].astype(F32)) * FACTOR).astype(BF16)
        dv_out[rows(j), :] = (v_sum[full, :] + v_near[rows(j), :].astype(F32)).astype(BF16)
        return carry

    for n, (first, size) in enumerate(BACK_PIECES):

        @pl.when(has_next)
        def _():
            took(near_back[n])

        lax.fori_loop(first // TILE, (first + size) // TILE, total, 0)

    gone(ins)

    @pl.when(has_next)
    def _():
        for copies in near_in + [far_in]:
            gone(copies)

    @pl.when(has_prev)
    def _():
        for copies in near_back + [far_back]:
            gone(copies)

    def finish(r, left):
        i = left % 8
        arrived(o_buf, i, o_recv)
        arrived(dq_buf, i, dq_recv)

        @pl.when(i != h)
        def _():
            for n in range(2):
                pltpu.make_async_copy(o_buf.at[i], o_buf.at[i], out_send.at[2 * r + n]).wait()

        return left // 8

    lax.fori_loop(0, 8, finish, code)


def local(seqs, queries, key_heads, value_heads, output_grad, doc_starts):
    vmem = pl.BlockSpec(memory_space=pltpu.VMEM)
    hbm = pl.BlockSpec(memory_space=pltpu.HBM)
    anywhere = pl.BlockSpec(memory_space=pl.ANY)
    dma = pltpu.SemaphoreType.DMA
    shapes = [jax.ShapeDtypeStruct(queries.shape, BF16)] * 2 + [jax.ShapeDtypeStruct(key_heads.shape, BF16)] * 2
    results = pl.pallas_call(
        functools.partial(kernel, seqs),
        out_shape=shapes,
        in_specs=[hbm] * 5,
        out_specs=[anywhere, anywhere, vmem, vmem],
        scratch_shapes=[pltpu.SMEM(doc_starts.shape, jnp.int32)]
        + [pltpu.VMEM((TILES, TILE, COLS), BF16)] * 4
        + [pltpu.VMEM((ROWS, HEAD), BF16)] * 2
        + [pltpu.VMEM((HEAD, ROWS), BF16)] * 2
        + [pltpu.VMEM((ROWS, HEAD), F32)] * 2
        + [pltpu.VMEM((WIN * TILE, COLS), F32)]
        + [pltpu.VMEM((WIN * TILE, COLS), BF16)] * 2
        + [pltpu.VMEM((BACK, HEAD), BF16)] * 2
        + [pltpu.VMEM((NEAR, HEAD), BF16)] * 2
        + [pltpu.VMEM((FAR, HEAD), BF16)] * 2
        + [dma((14,)), dma((8,)), dma((8,)), dma((16,)), dma((8,)), dma((8,)), dma((14,)), dma((19,))],
        compiler_params=pltpu.CompilerParams(
            collective_id=0, has_side_effects=True, vmem_limit_bytes=48 << 20
        ),
        cost_estimate=pl.CostEstimate(flops=10**10, bytes_accessed=8 << 20, transcendentals=6 << 20),
        name="attention",
    )(*(pltpu.with_memory_space_constraint(a, pltpu.HBM) for a in (doc_starts, queries, key_heads, value_heads, output_grad)))
    return results


def solution(mesh):
    wide = P(("seq", "head"), None)
    narrow = P("seq", "head")
    return jax.shard_map(
        functools.partial(local, mesh.shape["seq"]),
        mesh=mesh,
        in_specs=(wide, narrow, narrow, wide, P()),
        out_specs=(wide, wide, narrow, narrow),
        check_vma=False,
    )
```
